512 devices in a mesh: seq: 128 (over y, z, core), head: 4 (over x).
Axes of the slice: x: 4, y: 4, z: 16, core: 2. Of those that a mesh axis runs over, the one named last changes fastest.
Arguments:
- queries: bfloat16 [32768, 4096], P('seq', 'head'), may hold values from -6 to 6
- key_vectors: bfloat16 [32768, 4096], P('seq', 'head'), may hold values from -6 to 6
- value_vectors: bfloat16 [32768, 4096], P('seq', 'head'), may hold values from -6 to 6
- norm_gain: float32 [4096], P('head'), may hold values from 0.1 to 1.9
- out_weight: bfloat16 [4096, 4096], P('head', 'seq'), may hold values from -0.09375 to 0.09375
Outputs:
- projected: bfloat16 [32768, 4096], P('seq', 'head')
The draws below stay inside these ranges and needn't reach their ends.
All inputs are finite; a program needn't handle non-finite values.
Results may differ from the reference program's by a relative error of at most 0.022.
Values may be sent and summed in bfloat16 or wider, within the bound.
A program may use at most 192 MiB of HBM per device.

```python
import jax
import jax.numpy as jnp
from jax import lax

HEADS = 32
HD = 128
D = 4096
BLOCK = 256
TOKENS = 32768
N_HEAD = 4


def block_scale(stream_key, extent, cuts, least, largest):
    loudness, own = 1.0, jax.random.fold_in(stream_key, 6)
    for axis_at, shards_of in cuts:
        steps = jnp.exp(jax.random.uniform(jax.random.fold_in(own, axis_at), (shards_of,), jnp.float32, least / len(cuts), largest / len(cuts)))
        loudness = loudness * jnp.repeat(steps, extent[axis_at] // shards_of).reshape([-1 if axis == axis_at else 1 for axis in range(len(extent))])
    return loudness


def bell_draw(rng, extent, spread, reach, pieces=(), kind=jnp.bfloat16):
    loudness = block_scale(rng, extent, pieces, -0.22, 0.18) if pieces else 1.0
    drawn = jax.random.normal(rng, extent, jnp.float32) * spread * loudness
    return jnp.minimum(jnp.maximum(drawn, -reach), reach).astype(kind)


def setup_inputs(seed: int = 0) -> dict:
    streams_of = jax.random.split(jax.random.key(seed), 6)
    queries = bell_draw(streams_of[0], (TOKENS, HEADS * HD), 1.0, 6.0, ((0, 128), (1, 4)))
    key_vectors = bell_draw(streams_of[1], (TOKENS, HEADS * HD), 1.0, 6.0, ((0, 128), (1, 4)))
    value_vectors = bell_draw(streams_of[2], (TOKENS, HEADS * HD), 1.0, 6.0, ((0, 128), (1, 4)))
    norm_gain = jnp.clip(1.0 + 0.18 * jax.random.normal(streams_of[3], (HEADS * HD,), jnp.float32), 0.1, 1.9)
    out_weight = bell_draw(streams_of[4], (HEADS * HD, D), (HEADS * HD) ** -0.5, 0.09375, ((0, 4), (1, 128)))
    return {"queries": queries, "key_vectors": key_vectors, "value_vectors": value_vectors, "norm_gain": norm_gain, "out_weight": out_weight}


epsilon = 1e-06

def reference(queries, key_vectors, value_vectors, norm_gain, out_weight):
    block_count = TOKENS // BLOCK
    shape_four = (block_count, BLOCK, HEADS, HD)
    query_blocks = queries.reshape(shape_four)
    key_blocks = key_vectors.reshape(shape_four)
    value_blocks = value_vectors.reshape(shape_four)
    positions = jnp.arange(BLOCK, dtype=jnp.int32)
    causal = positions[:, None] >= positions[None, :]
    gain_table = norm_gain.reshape(HEADS, HD)

    def advance(state_now, inputs_now):
        query_now, key_now, value_now = inputs_now
        query_wide = query_now.astype(jnp.float32)
        key_wide = key_now.astype(jnp.float32)
        value_wide = value_now.astype(jnp.float32)
        scores = jnp.einsum('thd,shd->hts', query_wide, key_wide)
        scores = jnp.where(causal[None], scores, jnp.float32(0.0)).astype(jnp.bfloat16)
        within = jnp.einsum('hts,shd->thd', scores.astype(jnp.float32), value_wide)
        state_rounded = state_now.astype(jnp.bfloat16).astype(jnp.float32)
        carried = jnp.einsum('thd,hde->the', query_wide, state_rounded)
        combined = within + carried
        root_mean = jnp.sqrt(lax.optimization_barrier(jnp.mean(combined * combined, axis=-1, keepdims=True)) + epsilon)
        normed = (combined / root_mean * gain_table[None]).astype(jnp.bfloat16)
        block_term = jnp.einsum('thd,the->hde', key_wide, value_wide)
        return (state_now + block_term, normed.reshape(BLOCK, HEADS * HD))
    empty_state = jnp.zeros((HEADS, HD, HD), jnp.float32)
    _, attended = lax.scan(advance, empty_state, (query_blocks, key_blocks, value_blocks))
    attended = attended.reshape(TOKENS, HEADS * HD)
    group_rows = HEADS * HD // N_HEAD
    total = jnp.zeros((TOKENS, D), jnp.float32)
    for group in range(N_HEAD):
        lower = group * group_rows
        part = jnp.dot(attended[:, lower:lower + group_rows], out_weight[lower:lower + group_rows], preferred_element_type=jnp.float32).astype(jnp.bfloat16)
        part = lax.optimization_barrier(part)
        total = total + part.astype(jnp.float32)
    return total.astype(jnp.bfloat16)
```

```python
import jax
import jax.numpy as jnp
from jax import lax
from jax.experimental import pallas as pl
from jax.experimental.pallas import tpu as pltpu
from jax.sharding import PartitionSpec as P

HD = 128
NY, NZ, NX = 4, 16, 4
EPS = 1e-06
MESH = pl.DeviceIdType.MESH
TICKS = 9
CHUNKS = 4


def slots(tick):
    if tick == 0:
        return 0, 1
    if tick == 8:
        return 15, 1
    return 2 * tick - 1, 2


def kernel(
    q_hbm, k_hbm, v_hbm, gain_hbm, w_hbm, out_ref,
    q_v, k_v, v_v, gain_v, q_t, within, gain_t, t_own, t_send, t_sib, c_send, z_in, pre, y_in,
    p_out, p_half, s_send, s_all, att, w_buf, x1_send, x1_recv, x2_send, x2_recv, keep,
    load_sem, sib_sem, once_send, once_recv, wz_recv, wl_recv, wr_recv, w2_recv, ws_recv, w_send,
    x1_sem, x2_sem, x_send,
):
    s = lax.axis_index("seq")
    x = lax.axis_index("head")
    c = lax.rem(s, 2)
    z = lax.rem(s // 2, NZ)
    y = s // (2 * NZ)

    def at(dy=0, dz=0, dx=0, flip=False):
        yy, zz = lax.rem(y + dy + NY, NY), lax.rem(z + dz + NZ, NZ)
        return ((yy * NZ + zz) * 2 + (1 - c if flip else c), lax.rem(x + dx + NX, NX))

    def remote(src, dst, send, recv, device):
        return pltpu.make_async_remote_copy(
            src_ref=src, dst_ref=dst, send_sem=send, recv_sem=recv, device_id=device, device_id_type=MESH
        )

    def take(ref, sem):
        pltpu.make_async_copy(ref, ref, sem).wait()

    z_far = [8, 7, 9, 6, 10, 5, 11, 4, 12, 3, 13, 2, 14, 1, 15]
    barrier = pltpu.get_barrier_semaphore()
    partners = [at(dz=d) for d in z_far] + [at(dy=d) for d in (1, 2, 3)] + [at(dx=1), at(dx=-1), at(flip=True)]
    for partner in partners:
        pl.semaphore_signal(barrier, inc=1, device_id=partner, device_id_type=MESH)

    loads = [
        pltpu.make_async_copy(v_hbm, v_v, load_sem.at[0]),
        pltpu.make_async_copy(k_hbm, k_v, load_sem.at[1]),
        pltpu.make_async_copy(q_hbm, q_v, load_sem.at[2]),
        pltpu.make_async_copy(gain_hbm, gain_v, load_sem.at[3]),
        pltpu.make_async_copy(w_hbm, w_buf.at[y, 0, c], load_sem.at[4]),
    ]
    for load in loads:
        load.start()
    loads[0].wait()
    loads[1].wait()

    heads = q_v.shape[1] // HD
    half = heads * HD // 2
    for h in range(heads):
        cols = pl.ds(h * HD, HD)
        v_t = v_v[:, cols].T
        state = jnp.dot(v_t, k_v[:, cols], preferred_element_type=jnp.float32)
        t_own[cols, :] = state
        t_send[cols, :] = state.astype(jnp.bfloat16)
    loads[2].wait()
    loads[3].wait()
    loads[4].wait()

    pl.semaphore_wait(barrier, len(partners))

    mine = pl.ds(pl.multiple_of(c * half, half), half)
    other = pl.ds(pl.multiple_of((1 - c) * half, half), half)
    t_copy = remote(t_send.at[other], t_sib, sib_sem.at[0], sib_sem.at[1], at(flip=True))
    t_copy.start()

    rel = [y, lax.rem(y + NY - 1, NY), lax.rem(y + 1, NY), lax.rem(y + 2, NY)]

    def w_at(row, tick):
        first, count = slots(tick)
        return w_buf.at[rel[row], pl.ds(first, count), c]

    def to_sibling(row, tick):
        part = w_at(row, tick)
        remote(part, part, w_send.at[3], ws_recv.at[tick, row], at(flip=True)).start()

    def along_z(slot_from, slot_to, dz):
        remote(
            w_buf.at[y, slot_from, c], w_buf.at[y, slot_to, c], w_send.at[0], wz_recv.at[slot_to], at(dz=dz)
        ).start()

    def tick(k):
        if k == 0:
            along_z(0, 1, 1)
            along_z(0, 2, -1)
        elif k < TICKS:
            take(w_buf.at[y, 2 * k - 1, c], wz_recv.at[2 * k - 1])
            if k < 8:
                along_z(2 * k - 1, 2 * k + 1, 1)
                take(w_buf.at[y, 2 * k, c], wz_recv.at[2 * k])
            if k < 7:
                along_z(2 * k, 2 * k + 2, -1)
        if k < TICKS:
            part = w_at(0, k)
            remote(part, part, w_send.at[1], wl_recv.at[k], at(dy=1)).start()
            remote(part, part, w_send.at[1], wr_recv.at[k], at(dy=-1)).start()
            to_sibling(0, k)
        j = k - 1
        if 0 <= j < TICKS:
            first, count = slots(j)
            take(w_at(1, j), wl_recv.at[j])
            for slot in range(first, first + count):
                if slot % 2 == 0:
                    part = w_buf.at[rel[1], slot, c]
                    remote(part, part, w_send.at[2], w2_recv.at[slot], at(dy=1)).start()
            to_sibling(1, j)
            take(w_at(2, j), wr_recv.at[j])
            for slot in range(first, first + count):
                if slot % 2 == 1:
                    part = w_buf.at[rel[2], slot, c]
                    remote(part, part, w_send.at[2], w2_recv.at[slot], at(dy=-1)).start()
            to_sibling(2, j)
        j = k - 2
        if 0 <= j < TICKS:
            first, count = slots(j)
            for slot in range(first, first + count):
                take(w_buf.at[rel[3], slot, c], w2_recv.at[slot])
            to_sibling(3, j)

    tick(0)

    t_copy.wait_recv()
    c_send[...] = (t_own[mine, :] + t_sib[...].astype(jnp.float32)).astype(jnp.bfloat16).reshape(c_send.shape)
    for d in z_far:
        remote(
            c_send.at[lax.rem(z + d, NZ)], z_in.at[z], once_send.at[0], once_recv.at[0], at(dz=d)
        ).start()
    z_in[z] = c_send[z]

    before = lax.broadcasted_iota(jnp.int32, (256, 256), 0) <= lax.broadcasted_iota(jnp.int32, (256, 256), 1)
    for h in range(heads):
        cols = pl.ds(h * HD, HD)
        q_t[cols, :] = q_v[:, cols].T
        scores = jnp.dot(k_v[:, cols], q_t[cols, :], preferred_element_type=jnp.float32)
        scores = jnp.where(before, scores, 0.0).astype(jnp.bfloat16)
        v_t = v_v[:, cols].T
        within[cols, :] = jnp.dot(v_t, scores, preferred_element_type=jnp.float32)
        gain_t[cols, :] = jnp.broadcast_to(gain_v[h : h + 1, :], (HD, HD)).T

    tick(1)
    tick(2)

    take(z_in.at[pl.ds(0, NZ - 1)], once_recv.at[0])
    total = jnp.zeros(z_in.shape[1:], jnp.float32)
    for j in range(NZ):
        pre[j] = total
        total = total + z_in[j].astype(jnp.float32)
    y_in[y] = total.astype(jnp.bfloat16)
    for d in (2, 1, 3):
        remote(y_in.at[y], y_in.at[y], once_send.at[1], once_recv.at[1], at(dy=d)).start()
    tick(3)
    take(y_in.at[pl.ds(0, NY - 1)], once_recv.at[1])
    base = jnp.zeros(z_in.shape[1:], jnp.float32)
    for j in range(NY):
        base = base + jnp.where(j < y, y_in[j].astype(jnp.float32), 0.0)
    for j in range(NZ):
        p_out[j] = (base + pre[j]).astype(jnp.bfloat16)
    for d in z_far:
        remote(
            p_out.at[lax.rem(z + d, NZ)], p_half.at[z], once_send.at[2], once_recv.at[2], at(dz=d)
        ).start()
    p_half[z] = p_out[z]
    tick(4)
    tick(5)
    take(p_half.at[pl.ds(0, NZ - 1)], once_recv.at[2])
    prefix = p_half[...].astype(jnp.float32).reshape(half, HD)
    s_send[...] = (prefix + jnp.where(c == 0, t_own[mine, :], 0.0)).astype(jnp.bfloat16)
    s_copy = remote(s_send, s_all.at[mine], sib_sem.at[2], sib_sem.at[3], at(flip=True))
    s_copy.start()
    s_all[mine, :] = (prefix + jnp.where(c == 1, t_sib[...].astype(jnp.float32), 0.0)).astype(jnp.bfloat16)
    take(s_all.at[other], sib_sem.at[3])

    for h in range(heads):
        cols = pl.ds(h * HD, HD)
        combined = within[cols, :] + jnp.dot(s_all[cols, :], q_t[cols, :], preferred_element_type=jnp.float32)
        mean = jnp.mean(combined * combined, axis=0, keepdims=True)
        att[cols, :] = (combined * lax.rsqrt(mean + EPS) * gain_t[cols, 0:1]).astype(jnp.bfloat16)

    right, left, across = lax.rem(x + 1, NX), lax.rem(x + NX - 1, NX), lax.rem(x + 2, NX)

    def partial(dest, g):
        w = w_buf[dest, 4 * g : 4 * g + 4].reshape(256, w_buf.shape[-1])
        return jnp.dot(w, att[...], preferred_element_type=jnp.float32)

    def x2_start(g, way, part, dx):
        remote(
            x2_send.at[g, way, part], x2_recv.at[g, way, part], x_send, x2_sem.at[g, way, part], at(dx=dx)
        ).start()

    def project(g):
        for t in ((0, 1, 2), (3, 4), (5, 6), (7, 8))[g]:
            for row in range(4):
                first, count = slots(t)
                take(w_buf.at[rel[row], pl.ds(first, count), 1 - c], ws_recv.at[t, row])
        far = partial(across, g).astype(jnp.bfloat16).reshape(2, 128, 256)
        for way, dx in ((0, 1), (1, -1)):
            x1_send[g, way] = far[way]
            remote(x1_send.at[g, way], x1_recv.at[g, way], x_send, x1_sem.at[g, way], at(dx=dx)).start()
        near = partial(right, g)
        x2_send[g, 0, 1] = near[128:].astype(jnp.bfloat16)
        x2_start(g, 0, 1, 1)
        keep[g, 0] = near[:128]
        near = partial(left, g)
        x2_send[g, 1, 0] = near[:128].astype(jnp.bfloat16)
        x2_start(g, 1, 0, -1)
        keep[g, 1] = near[128:]
        own = partial(x, g)
        keep[g, 2] = own[:128]
        keep[g, 3] = own[128:]

    def join(g):
        for way, dx in ((0, 1), (1, -1)):
            take(x1_recv.at[g, way], x1_sem.at[g, way])
            x2_send[g, way, way] = (keep[g, way] + x1_recv[g, way].astype(jnp.float32)).astype(jnp.bfloat16)
            x2_start(g, way, way, dx)

    def finish(g):
        for way, part in ((0, 1), (1, 0), (0, 0), (1, 1)):
            take(x2_recv.at[g, way, part], x2_sem.at[g, way, part])
        for part in range(2):
            total = keep[g, 2 + part] + (
                x2_recv[g, 0, part].astype(jnp.float32) + x2_recv[g, 1, part].astype(jnp.float32)
            )
            total = total.astype(jnp.bfloat16)
            for i in range(2):
                slot = 4 * g + 2 * part + i
                step = (slot + 1) // 2
                where = lax.rem(z + (NZ - step if slot % 2 == 1 else step), NZ)
                out_ref[pl.ds(pl.multiple_of(where * 64, 64), 64), :] = total[64 * i : 64 * i + 64]

    project(0)
    tick(6)
    project(1)
    join(0)
    tick(7)
    tick(8)
    project(2)
    join(1)
    finish(0)
    tick(9)
    tick(10)
    project(3)
    join(2)
    finish(1)
    join(3)
    finish(2)
    finish(3)

    t_copy.wait_send()
    s_copy.wait_send()
    take(z_in.at[pl.ds(0, NZ - 1)], once_send.at[0])
    take(y_in.at[pl.ds(0, NY - 1)], once_send.at[1])
    take(p_half.at[pl.ds(0, NZ - 1)], once_send.at[2])
    take(w_buf.at[0, pl.ds(0, 15), 0], w_send.at[0])
    take(w_buf.at[pl.ds(0, 2), pl.ds(0, 16), 0], w_send.at[1])
    take(w_buf.at[0, pl.ds(0, 16), 0], w_send.at[2])
    take(w_buf.at[pl.ds(0, 4), pl.ds(0, 16), 0], w_send.at[3])
    take(w_buf.at[0, pl.ds(0, 12), pl.ds(0, 2)], x_send)


def body(queries, key_vectors, value_vectors, norm_gain, out_weight):
    tokens, features = queries.shape
    heads = features // HD
    half = features // 2
    bf16, f32 = jnp.bfloat16, jnp.float32
    sem = pltpu.SemaphoreType.DMA
    anywhere = pl.BlockSpec(memory_space=pl.ANY)
    out = pl.pallas_call(
        kernel,
        out_shape=jax.ShapeDtypeStruct((features, tokens), bf16),
        in_specs=[anywhere] * 5,
        out_specs=pl.BlockSpec(memory_space=pltpu.VMEM),
        scratch_shapes=[
            pltpu.VMEM((tokens, features), bf16),
            pltpu.VMEM((tokens, features), bf16),
            pltpu.VMEM((tokens, features), bf16),
            pltpu.VMEM((heads, HD), f32),
            pltpu.VMEM((features, tokens), bf16),
            pltpu.VMEM((features, tokens), f32),
            pltpu.VMEM((features, HD), f32),
            pltpu.VMEM((features, HD), f32),
            pltpu.VMEM((features, HD), bf16),
            pltpu.VMEM((half, HD), bf16),
            pltpu.VMEM((NZ, half // NZ, HD), bf16),
            pltpu.VMEM((NZ, half // NZ, HD), bf16),
            pltpu.VMEM((NZ, half // NZ, HD), f32),
            pltpu.VMEM((NY, half // NZ, HD), bf16),
            pltpu.VMEM((NZ, half // NZ, HD), bf16),
            pltpu.VMEM((NZ, half // NZ, HD), bf16),
            pltpu.VMEM((half, HD), bf16),
            pltpu.VMEM((features, HD), bf16),
            pltpu.VMEM((features, tokens), bf16),
            pltpu.VMEM((NY, NZ, 2, 32, features), bf16),
            pltpu.VMEM((CHUNKS, 2, 128, tokens), bf16),
            pltpu.VMEM((CHUNKS, 2, 128, tokens), bf16),
            pltpu.VMEM((CHUNKS, 2, 2, 128, tokens), bf16),
            pltpu.VMEM((CHUNKS, 2, 2, 128, tokens), bf16),
            pltpu.VMEM((CHUNKS, 4, 128, tokens), f32),
            sem((5,)),
            sem((4,)),
            sem((3,)),
            sem((3,)),
            sem((16,)),
            sem((TICKS,)),
            sem((TICKS,)),
            sem((16,)),
            sem((TICKS, 4)),
            sem((4,)),
            sem((CHUNKS, 2)),
            sem((CHUNKS, 2, 2)),
            sem,
        ],
        compiler_params=pltpu.CompilerParams(
            collective_id=0, has_side_effects=True, vmem_limit_bytes=48 << 20
        ),
        cost_estimate=pl.CostEstimate(flops=2_550_000_000, bytes_accessed=12_000_000, transcendentals=4096),
        name="attend_and_project",
    )(queries, key_vectors, value_vectors, norm_gain.reshape(heads, HD), out_weight.T)
    return out.T


def solution(mesh):
    in_specs = (P("seq", "head"), P("seq", "head"), P("seq", "head"), P("head"), P("head", "seq"))
    return jax.shard_map(body, mesh=mesh, in_specs=in_specs, out_specs=P("seq", "head"), check_vma=False)
```

```python
import jax
import jax.numpy as jnp
from jax import lax
from jax.experimental import pallas as pl
from jax.experimental.pallas import tpu as pltpu
from jax.sharding import PartitionSpec as P

HD = 128
NY, NZ, NX = 4, 16, 4
EPS = 1e-06
MESH = pl.DeviceIdType.MESH
TICKS = 9
LAG_NEAR, LAG_FAR = 2, 4
KA = 768
LAG_PART = 2
CHUNKS = ((0, 4), (4, 4), (8, 4), (12, 3), (15, 1))
LAST_EARLY = 8


def slots(tick):
    if tick == 0:
        return 0, 1
    if tick == 8:
        return 15, 1
    return 2 * tick - 1, 2


def kernel(
    q_hbm, k_hbm, v_hbm, gain_hbm, w_hbm, out_ref,
    q_v, k_v, v_v, gain_v, q_t, within, gain_t, t_own, t_send, t_sib, c_send, z_in, pre, y_in,
    p_out, p_half, s_send, s_all, att, wa, wb, x1_send, x1_recv, x2_send, x2_recv, keep,
    load_sem, sib_sem, own_sem, once_send, once_recv, wz_recv, wl_recv, wr_recv, w2_recv, ws_recv, w_send,
    b_recv, bz_recv, bs_recv, b_send, x1_sem, x2_sem, x_send,
):
    s = lax.axis_index("seq")
    x = lax.axis_index("head")
    c = lax.rem(s, 2)
    z = lax.rem(s // 2, NZ)
    y = s // (2 * NZ)

    def at(dy=0, dz=0, dx=0, flip=False):
        yy, zz = lax.rem(y + dy + NY, NY), lax.rem(z + dz + NZ, NZ)
        return ((yy * NZ + zz) * 2 + (1 - c if flip else c), lax.rem(x + dx + NX, NX))

    def remote(src, dst, send, recv, device):
        return pltpu.make_async_remote_copy(
            src_ref=src, dst_ref=dst, send_sem=send, recv_sem=recv, device_id=device, device_id_type=MESH
        )

    def take(ref, sem):
        pltpu.make_async_copy(ref, ref, sem).wait()

    z_far = [8, 7, 9, 6, 10, 5, 11, 4, 12, 3, 13, 2, 14, 1, 15]
    barrier = pltpu.get_barrier_semaphore()
    near = [at(dz=1), at(dz=-1), at(dy=1), at(dy=2), at(dy=3), at(dx=1), at(dx=-1), at(flip=True)]
    far = [at(dz=d) for d in z_far if 1 < d < NZ - 1]

    def greet(partners):
        for partner in partners:
            pl.semaphore_signal(barrier, inc=1, device_id=partner, device_id_type=MESH)

    @pl.when(c == 0)
    def _():
        greet(far)

    greet(near)

    own_rows = pl.ds(pl.multiple_of(c * 32, 32), 32)
    loads = [
        pltpu.make_async_copy(v_hbm, v_v, load_sem.at[0]),
        pltpu.make_async_copy(k_hbm, k_v, load_sem.at[1]),
        pltpu.make_async_copy(q_hbm, q_v, load_sem.at[2]),
        pltpu.make_async_copy(gain_hbm, gain_v, load_sem.at[3]),
        pltpu.make_async_copy(w_hbm.at[:, pl.ds(0, KA)], wa.at[y, 0, own_rows], load_sem.at[4]),
        pltpu.make_async_copy(w_hbm.at[:, pl.ds(KA, wb.shape[-1])], wb.at[y, 0, own_rows], load_sem.at[5]),
    ]
    for load in loads:
        load.start()
    own_copies = [
        remote(w.at[y, 0, own_rows], w.at[y, 0, own_rows], own_sem.at[i], own_sem.at[2 + i], at(flip=True))
        for i, w in enumerate((wa, wb))
    ]

    def share_own(partners):
        loads[4].wait()
        loads[5].wait()
        pl.semaphore_wait(barrier, partners)
        for copy in own_copies:
            copy.start()

    rel = [y, lax.rem(y + NY - 1, NY), lax.rem(y + 1, NY), lax.rem(y + 2, NY)]

    part_rows = (pl.ds(32, 32), pl.ds(0, 32))

    def w_at(row, tick, part):
        first, count = slots(tick)
        return wa.at[rel[row], pl.ds(first, count), part_rows[part]]

    def to_sibling(row, tick, part):
        w = w_at(row, tick, part)
        remote(w, w, w_send.at[3 if row else 4], ws_recv.at[tick, row, part], at(flip=True)).start()

    def along_z(slot_from, slot_to, dz, part):
        rows = part_rows[part]
        remote(
            wa.at[y, slot_from, rows], wa.at[y, slot_to, rows], w_send.at[0], wz_recv.at[slot_to, part], at(dz=dz)
        ).start()

    def ring_tick(k, part):
        if k == 0:
            along_z(0, 1, 1, part)
            along_z(0, 2, -1, part)
        elif 0 < k < TICKS:
            take(wa.at[y, 2 * k - 1, part_rows[part]], wz_recv.at[2 * k - 1, part])
            if k < 8:
                along_z(2 * k - 1, 2 * k + 1, 1, part)
                take(wa.at[y, 2 * k, part_rows[part]], wz_recv.at[2 * k, part])
            if k < 7:
                along_z(2 * k, 2 * k + 2, -1, part)

    def row_tick(k, part):
        if 0 <= k < TICKS:
            w = w_at(0, k, part)
            remote(w, w, w_send.at[1], wl_recv.at[k, part], at(dy=1)).start()
            remote(w, w, w_send.at[1], wr_recv.at[k, part], at(dy=-1)).start()
            if k:
                to_sibling(0, k, part)
        j = k - LAG_NEAR
        if 0 <= j < TICKS:
            first, count = slots(j)
            take(w_at(1, j, part), wl_recv.at[j, part])
            for slot in range(first, first + count):
                if slot % 2 == 0:
                    w = wa.at[rel[1], slot, part_rows[part]]
                    remote(w, w, w_send.at[2], w2_recv.at[slot, part], at(dy=1)).start()
            to_sibling(1, j, part)
            take(w_at(2, j, part), wr_recv.at[j, part])
            for slot in range(first, first + count):
                if slot % 2 == 1:
                    w = wa.at[rel[2], slot, part_rows[part]]
                    remote(w, w, w_send.at[2], w2_recv.at[slot, part], at(dy=-1)).start()
            to_sibling(2, j, part)
        j = k - LAG_FAR
        if 0 <= j < TICKS:
            first, count = slots(j)
            for slot in range(first, first + count):
                take(wa.at[rel[3], slot, part_rows[part]], w2_recv.at[slot, part])
            to_sibling(3, j, part)

    all_rows = pl.ds(0, NY)

    def quad_start(part):
        own = wb.at[y, 0, part_rows[part]]
        for d in (1, 3, 2):
            remote(own, own, b_send.at[0], b_recv.at[part], at(dy=d)).start()

    def quad(slot_from, slot_to, dz, part):
        rows = part_rows[part]
        remote(
            wb.at[all_rows, slot_from, rows], wb.at[all_rows, slot_to, rows],
            b_send.at[1], bz_recv.at[slot_to, part], at(dz=dz),
        ).start()

    def quad_tick(k, part):
        rows = part_rows[part]
        if k == 0:
            take(wb.at[pl.ds(0, NY - 1), 0, rows], b_recv.at[part])
            quad(0, 1, 1, part)
            quad(0, 2, -1, part)
            for row in (1, 2, 3):
                w = wb.at[rel[row], 0, rows]
                remote(w, w, b_send.at[3], bs_recv.at[k, part], at(flip=True)).start()
        elif 0 < k < TICKS:
            take(wb.at[all_rows, 2 * k - 1, rows], bz_recv.at[2 * k - 1, part])
            if k < 8:
                quad(2 * k - 1, 2 * k + 1, 1, part)
                take(wb.at[all_rows, 2 * k, rows], bz_recv.at[2 * k, part])
            if k < 7:
                quad(2 * k, 2 * k + 2, -1, part)
            first, count = slots(k)
            w = wb.at[all_rows, pl.ds(first, count), rows]
            remote(w, w, b_send.at[2], bs_recv.at[k, part], at(flip=True)).start()

    def both(k):
        if k == LAG_PART:
            for copy in own_copies:
                copy.wait_recv()
        ring_tick(k, 0)
        ring_tick(k - LAG_PART, 1)
        if k == 0:
            quad_start(0)
        if k == LAG_PART:
            quad_start(1)
        quad_tick(k - 1, 0)
        quad_tick(k - LAG_PART - 1, 1)
        row_tick(k, 0)
        row_tick(k - LAG_PART, 1)

    @pl.when(c == 1)
    def _():
        share_own(len(near))
        both(0)

    loads[0].wait()
    loads[1].wait()

    heads = q_v.shape[1] // HD
    for h in range(heads):
        cols = pl.ds(h * HD, HD)
        v_t = v_v[:, cols].T
        state = jnp.dot(v_t, k_v[:, cols], preferred_element_type=jnp.float32)
        t_own[cols, :] = state
        t_send[cols, :] = state.astype(jnp.bfloat16)

    t_copy = remote(t_send, t_sib, sib_sem.at[0], sib_sem.at[1], at(flip=True))
    s_copy = remote(s_send, s_all, sib_sem.at[2], sib_sem.at[3], at(flip=True))

    before = lax.broadcasted_iota(jnp.int32, (256, 256), 0) <= lax.broadcasted_iota(jnp.int32, (256, 256), 1)

    def inside(h):
        cols = pl.ds(h * HD, HD)
        q_t[cols, :] = q_v[:, cols].T
        scores = jnp.dot(k_v[:, cols], q_t[cols, :], preferred_element_type=jnp.float32)
        scores = jnp.where(before, scores, 0.0).astype(jnp.bfloat16)
        v_t = v_v[:, cols].T
        within[cols, :] = jnp.dot(v_t, scores, preferred_element_type=jnp.float32)
        gain_t[cols, :] = jnp.broadcast_to(gain_v[h : h + 1, :], (HD, HD)).T

    half = heads // 2

    @pl.when(c == 1)
    def _():
        t_copy.start()
        both(1)

    @pl.when(c == 0)
    def _():
        share_own(len(near) + len(far))
        t_copy.wait_recv()
        c_send[...] = (t_own[...] + t_sib[...].astype(jnp.float32)).astype(jnp.bfloat16).reshape(c_send.shape)
        for d in z_far:
            remote(
                c_send.at[lax.rem(z + d, NZ)], z_in.at[z], once_send.at[0], once_recv.at[0], at(dz=d)
            ).start()
        z_in[z] = c_send[z]

    loads[2].wait()
    loads[3].wait()
    for h in range(half):
        inside(h)

    @pl.when(c == 1)
    def _():
        both(2)

    for h in range(half, heads):
        inside(h)

    @pl.when(c == 1)
    def _():
        for k in range(3, LAST_EARLY + 1):
            both(k)
        s_copy.wait_recv()

    @pl.when(c == 0)
    def _():
        take(z_in.at[pl.ds(0, NZ - 1)], once_recv.at[0])
        total = jnp.zeros(z_in.shape[1:], jnp.float32)
        for j in range(NZ):
            pre[j] = total
            total = total + z_in[j].astype(jnp.float32)
        y_in[y] = total.astype(jnp.bfloat16)
        for d in (2, 1, 3):
            remote(y_in.at[y], y_in.at[y], once_send.at[1], once_recv.at[1], at(dy=d)).start()
        take(y_in.at[pl.ds(0, NY - 1)], once_recv.at[1])
        base = jnp.zeros(z_in.shape[1:], jnp.float32)
        for j in range(NY):
            base = base + jnp.where(j < y, y_in[j].astype(jnp.float32), 0.0)
        for j in range(NZ):
            p_out[j] = (base + pre[j]).astype(jnp.bfloat16)
        for d in z_far:
            remote(
                p_out.at[lax.rem(z + d, NZ)], p_half.at[z], once_send.at[2], once_recv.at[2], at(dz=d)
            ).start()
        p_half[z] = p_out[z]
        take(p_half.at[pl.ds(0, NZ - 1)], once_recv.at[2])
        prefix = p_half[...].reshape(s_all.shape)
        s_send[...] = (prefix.astype(jnp.float32) + t_own[...]).astype(jnp.bfloat16)
        s_copy.start()
        s_all[...] = prefix
        for copy in own_copies:
            copy.wait_recv()

    for h in range(heads):
        cols = pl.ds(h * HD, HD)
        combined = within[cols, :] + jnp.dot(s_all[cols, :], q_t[cols, :], preferred_element_type=jnp.float32)
        mean = jnp.mean(combined * combined, axis=0, keepdims=True)
        att[cols, :] = (combined * lax.rsqrt(mean + EPS) * gain_t[cols, 0:1]).astype(jnp.bfloat16)

    right, left, across = lax.rem(x + 1, NX), lax.rem(x + NX - 1, NX), lax.rem(x + 2, NX)

    def partial(dest, g):
        first, count = CHUNKS[g]
        a = wa[dest, first : first + count].reshape(64 * count, KA)
        b = wb[dest, first : first + count].reshape(64 * count, wb.shape[-1])
        return jnp.dot(a, att[:KA, :], preferred_element_type=jnp.float32) + jnp.dot(
            b, att[KA:, :], preferred_element_type=jnp.float32
        )

    def x_rows(g):
        first, count = CHUNKS[g]
        return pl.ds(32 * first, 32 * count), 32 * count

    def x2_start(g, way, part, dx):
        rows, _ = x_rows(g)
        remote(
            x2_send.at[way, part, rows], x2_recv.at[way, part, rows], x_send.at[1], x2_sem.at[g, way, part], at(dx=dx)
        ).start()

    def last_tick(g):
        return (CHUNKS[g][0] + CHUNKS[g][1]) // 2

    def arrived(g):
        for t in range(last_tick(g - 1) + 1 if g else 0, last_tick(g) + 1):
            first, count = slots(t)
            for part, rows in enumerate(part_rows):
                take(wb.at[pl.ds(0, NY if t else NY - 1), pl.ds(first, count), rows], bs_recv.at[t, part])
                for row in range(0 if t else 1, 4):
                    take(w_at(row, t, part), ws_recv.at[t, row, part])

    def project(g):
        rows, half_rows = x_rows(g)
        opposite = partial(across, g).astype(jnp.bfloat16)
        for way, dx in ((0, 1), (1, -1)):
            x1_send[way, rows] = opposite[way * half_rows : (way + 1) * half_rows]
            remote(
                x1_send.at[way, rows], x1_recv.at[way, rows], x_send.at[0], x1_sem.at[g, way], at(dx=dx)
            ).start()
        near = partial(right, g)
        x2_send[0, 1, rows] = near[half_rows:].astype(jnp.bfloat16)
        x2_start(g, 0, 1, 1)
        keep[0, rows] = near[:half_rows]
        near = partial(left, g)
        x2_send[1, 0, rows] = near[:half_rows].astype(jnp.bfloat16)
        x2_start(g, 1, 0, -1)
        keep[1, rows] = near[half_rows:]
        own = partial(x, g)
        keep[2, rows] = own[:half_rows]
        keep[3, rows] = own[half_rows:]

    def join(g):
        rows, _ = x_rows(g)
        for way, dx in ((0, 1), (1, -1)):
            take(x1_recv.at[way, rows], x1_sem.at[g, way])
            x2_send[way, way, rows] = (keep[way, rows] + x1_recv[way, rows].astype(jnp.float32)).astype(jnp.bfloat16)
            x2_start(g, way, way, dx)

    def finish(g):
        rows, half_rows = x_rows(g)
        for way, part in ((0, 1), (1, 0), (0, 0), (1, 1)):
            take(x2_recv.at[way, part, rows], x2_sem.at[g, way, part])
        for part in range(2):
            total = keep[2 + part, rows] + (
                x2_recv[0, part, rows].astype(jnp.float32) + x2_recv[1, part, rows].astype(jnp.float32)
            )
            total = total.astype(jnp.bfloat16)
            for i in range(half_rows // 32):
                unit = 2 * CHUNKS[g][0] + part * (half_rows // 32) + i
                slot, core = unit // 2, unit % 2
                step = (slot + 1) // 2
                where = lax.rem(z + (NZ - step if slot % 2 == 1 else step), NZ)
                out_ref[pl.ds(pl.multiple_of(where * 64 + core * 32, 32), 32), :] = total[32 * i : 32 * i + 32]

    done = LAST_EARLY
    count = len(CHUNKS)
    for g in range(count):
        need = max(done, last_tick(g) + LAG_PART + LAG_FAR)

        @pl.when(c == 1)
        def _():
            for k in range(done + 1, need + 1):
                both(k)

        @pl.when(c == 0)
        def _():
            arrived(g)

        done = need
        project(g)
        if g >= 1:
            join(g - 1)
        if g >= 2:
            finish(g - 2)
    join(count - 1)
    finish(count - 2)
    finish(count - 1)

    for copy in own_copies:
        copy.wait_send()
    take(x1_recv, x_send.at[0])
    take(x2_recv, x_send.at[1])

    @pl.when(c == 0)
    def _():
        s_copy.wait_send()
        take(z_in.at[pl.ds(0, NZ - 1)], once_send.at[0])
        take(y_in.at[pl.ds(0, NY - 1)], once_send.at[1])
        take(p_half.at[pl.ds(0, NZ - 1)], once_send.at[2])

    @pl.when(c == 1)
    def _():
        t_copy.wait_send()
        take(wa.at[0, pl.ds(0, 15)], w_send.at[0])
        take(wa.at[pl.ds(0, 2)], w_send.at[1])
        take(wa.at[0], w_send.at[2])
        take(wa.at[pl.ds(0, 3)], w_send.at[3])
        take(wa.at[0, pl.ds(0, 15)], w_send.at[4])
        take(wb.at[pl.ds(0, NY - 1), 0], b_send.at[0])
        take(wb.at[:, pl.ds(0, 15)], b_send.at[1])
        take(wb.at[pl.ds(0, NY - 1), 0], b_send.at[3])
        take(wb.at[:, pl.ds(0, 15)], b_send.at[2])


def body(queries, key_vectors, value_vectors, norm_gain, out_weight):
    tokens, features = queries.shape
    heads = features // HD
    bf16, f32 = jnp.bfloat16, jnp.float32
    sem = pltpu.SemaphoreType.DMA
    anywhere = pl.BlockSpec(memory_space=pl.ANY)
    out = pl.pallas_call(
        kernel,
        out_shape=jax.ShapeDtypeStruct((features, tokens), bf16),
        in_specs=[anywhere] * 5,
        out_specs=pl.BlockSpec(memory_space=pltpu.VMEM),
        scratch_shapes=[
            pltpu.VMEM((tokens, features), bf16),
            pltpu.VMEM((tokens, features), bf16),
            pltpu.VMEM((tokens, features), bf16),
            pltpu.VMEM((heads, HD), f32),
            pltpu.VMEM((features, tokens), bf16),
            pltpu.VMEM((features, tokens), f32),
            pltpu.VMEM((features, HD), f32),
            pltpu.VMEM((features, HD), f32),
            pltpu.VMEM((features, HD), bf16),
            pltpu.VMEM((features, HD), bf16),
            pltpu.VMEM((NZ, features // NZ, HD), bf16),
            pltpu.VMEM((NZ, features // NZ, HD), bf16),
            pltpu.VMEM((NZ, features // NZ, HD), f32),
            pltpu.VMEM((NY, features // NZ, HD), bf16),
            pltpu.VMEM((NZ, features // NZ, HD), bf16),
            pltpu.VMEM((NZ, features // NZ, HD), bf16),
            pltpu.VMEM((features, HD), bf16),
            pltpu.VMEM((features, HD), bf16),
            pltpu.VMEM((features, tokens), bf16),
            pltpu.VMEM((NY, NZ, 64, KA), bf16),
            pltpu.VMEM((NY, NZ, 64, features - KA), bf16),
            pltpu.VMEM((2, features // 2, tokens), bf16),
            pltpu.VMEM((2, features // 2, tokens), bf16),
            pltpu.VMEM((2, 2, features // 2, tokens), bf16),
            pltpu.VMEM((2, 2, features // 2, tokens), bf16),
            pltpu.VMEM((4, features // 2, tokens), f32),
            sem((6,)),
            sem((4,)),
            sem((4,)),
            sem((3,)),
            sem((3,)),
            sem((16, 2)),
            sem((TICKS, 2)),
            sem((TICKS, 2)),
            sem((16, 2)),
            sem((TICKS, 4, 2)),
            sem((5,)),
            sem((2,)),
            sem((16, 2)),
            sem((TICKS, 2)),
            sem((4,)),
            sem((len(CHUNKS), 2)),
            sem((len(CHUNKS), 2, 2)),
            sem((2,)),
        ],
        compiler_params=pltpu.CompilerParams(
            collective_id=0, has_side_effects=True, vmem_limit_bytes=62 << 20
        ),
        cost_estimate=pl.CostEstimate(flops=2_550_000_000, bytes_accessed=12_000_000, transcendentals=4096),
        name="attend_and_project",
    )(queries, key_vectors, value_vectors, norm_gain.reshape(heads, HD), out_weight.T)
    return out.T


def solution(mesh):
    in_specs = (P("seq", "head"), P("seq", "head"), P("seq", "head"), P("head"), P("head", "seq"))
    return jax.shard_map(body, mesh=mesh, in_specs=in_specs, out_specs=P("seq", "head"), check_vma=False)
```

```python
import jax
import jax.numpy as jnp
from jax import lax
from jax.experimental import pallas as pl
from jax.experimental.pallas import tpu as pltpu
from jax.sharding import PartitionSpec as P

HD = 128
NY, NZ, NX = 4, 16, 4
EPS = 1e-06
MESH = pl.DeviceIdType.MESH
PAIRS = NZ // 2
TICKS = 9
LAG_NEAR, LAG_FAR = 2, 4
KA = 768
LAG_PART = 2
LONG_WAY = 1
CHUNKS = ((0, 4), (4, 4), (8, 4), (12, 3), (15, 1))
LAST_EARLY = 10


def slots(tick):
    if tick == 0:
        return 0, 1
    if tick == 8:
        return 15, 1
    return 2 * tick - 1, 2


def kernel(
    q_hbm, k_hbm, v_hbm, gain_hbm, w_hbm, out_ref,
    q_v, k_v, v_v, gain_v, q_t, within, gain_t, t_own, t_send, t_sib, chip, pair_send, pair_in, back_send, s_pre, c_send, z_in, pre, y_in,
    p_out, p_half, s_send, s_all, att, wa, wb, x1_send, x1_recv, x2_send, x2_recv, keep, out_t,
    load_sem, sib_sem, own_sem, pair_sem, once_send, once_recv, wz_recv, wl_recv, wr_recv, w2_recv, ws_recv, w_send,
    b_recv, bz_recv, bs_recv, b_send, x1_sem, x2_sem, x_send,
):
    s = lax.axis_index("seq")
    x = lax.axis_index("head")
    c = lax.rem(s, 2)
    z = lax.rem(s // 2, NZ)
    y = s // (2 * NZ)

    def at(dy=0, dz=0, dx=0, flip=False):
        yy, zz = lax.rem(y + dy + NY, NY), lax.rem(z + dz + NZ, NZ)
        return ((yy * NZ + zz) * 2 + (1 - c if flip else c), lax.rem(x + dx + NX, NX))

    def remote(src, dst, send, recv, device):
        return pltpu.make_async_remote_copy(
            src_ref=src, dst_ref=dst, send_sem=send, recv_sem=recv, device_id=device, device_id_type=MESH
        )

    def take(ref, sem):
        pltpu.make_async_copy(ref, ref, sem).wait()

    pair_far = [8, 6, 10, 4, 12, 2, 14]
    barrier = pltpu.get_barrier_semaphore()
    near = [at(dz=1), at(dz=-1), at(dy=1), at(dy=2), at(dy=3), at(dx=1), at(dx=-1), at(flip=True)]
    far = [at(dz=d) for d in pair_far]

    def greet(partners):
        for partner in partners:
            pl.semaphore_signal(barrier, inc=1, device_id=partner, device_id_type=MESH)

    @pl.when(c == 0)
    def _():
        greet(far)

    greet(near)

    own_rows = pl.ds(pl.multiple_of(c * 32, 32), 32)
    loads = [
        pltpu.make_async_copy(v_hbm, v_v, load_sem.at[0]),
        pltpu.make_async_copy(k_hbm, k_v, load_sem.at[1]),
        pltpu.make_async_copy(q_hbm, q_v, load_sem.at[2]),
        pltpu.make_async_copy(gain_hbm, gain_v, load_sem.at[3]),
        pltpu.make_async_copy(w_hbm.at[:, pl.ds(0, KA)], wa.at[y, 0, own_rows], load_sem.at[4]),
        pltpu.make_async_copy(w_hbm.at[:, pl.ds(KA, wb.shape[-1])], wb.at[y, 0, own_rows], load_sem.at[5]),
    ]
    for load in loads:
        load.start()
    own_copies = [
        remote(w.at[y, 0, own_rows], w.at[y, 0, own_rows], own_sem.at[i], own_sem.at[2 + i], at(flip=True))
        for i, w in enumerate((wa, wb))
    ]

    def share_own(partners):
        loads[4].wait()
        loads[5].wait()
        pl.semaphore_wait(barrier, partners)
        for copy in own_copies:
            copy.start()

    rel = [y, lax.rem(y + NY - 1, NY), lax.rem(y + 1, NY), lax.rem(y + 2, NY)]

    part_rows = (pl.ds(32, 32), pl.ds(0, 32))

    def w_at(row, tick, part):
        first, count = slots(tick)
        return wa.at[rel[row], pl.ds(first, count), part_rows[part]]

    def to_sibling(row, tick, part):
        w = w_at(row, tick, part)
        remote(w, w, w_send.at[3 if row else 4], ws_recv.at[tick, row, part], at(flip=True)).start()

    def along_z(slot_from, slot_to, dz, part):
        rows = part_rows[part]
        remote(
            wa.at[y, slot_from, rows], wa.at[y, slot_to, rows], w_send.at[0], wz_recv.at[slot_to, part], at(dz=dz * LONG_WAY)
        ).start()

    def ring_tick(k, part):
        if k == 0:
            along_z(0, 1, 1, part)
            along_z(0, 2, -1, part)
        elif 0 < k < TICKS:
            take(wa.at[y, 2 * k - 1, part_rows[part]], wz_recv.at[2 * k - 1, part])
            if k < 8:
                along_z(2 * k - 1, 2 * k + 1, 1, part)
                take(wa.at[y, 2 * k, part_rows[part]], wz_recv.at[2 * k, part])
            if k < 7:
                along_z(2 * k, 2 * k + 2, -1, part)

    def row_tick(k, part):
        if 0 <= k < TICKS:
            w = w_at(0, k, part)
            remote(w, w, w_send.at[1], wl_recv.at[k, part], at(dy=1)).start()
            remote(w, w, w_send.at[1], wr_recv.at[k, part], at(dy=-1)).start()
            if k:
                to_sibling(0, k, part)
        j = k - LAG_NEAR
        if 0 <= j < TICKS:
            first, count = slots(j)
            take(w_at(1, j, part), wl_recv.at[j, part])
            for slot in range(first, first + count):
                if slot % 2 == 0:
                    w = wa.at[rel[1], slot, part_rows[part]]
                    remote(w, w, w_send.at[2], w2_recv.at[slot, part], at(dy=1)).start()
            to_sibling(1, j, part)
            take(w_at(2, j, part), wr_recv.at[j, part])
            for slot in range(first, first + count):
                if slot % 2 == 1:
                    w = wa.at[rel[2], slot, part_rows[part]]
                    remote(w, w, w_send.at[2], w2_recv.at[slot, part], at(dy=-1)).start()
            to_sibling(2, j, part)
        j = k - LAG_FAR
        if 0 <= j < TICKS:
            first, count = slots(j)
            for slot in range(first, first + count):
                take(wa.at[rel[3], slot, part_rows[part]], w2_recv.at[slot, part])
            to_sibling(3, j, part)

    all_rows = pl.ds(0, NY)

    def quad_start(part):
        own = wb.at[y, 0, part_rows[part]]
        for d in (1, 3, 2):
            remote(own, own, b_send.at[0], b_recv.at[part], at(dy=d)).start()

    def quad(slot_from, slot_to, dz, part):
        rows = part_rows[part]
        remote(
            wb.at[all_rows, slot_from, rows], wb.at[all_rows, slot_to, rows],
            b_send.at[1], bz_recv.at[slot_to, part], at(dz=dz * LONG_WAY),
        ).start()

    def quad_tick(k, part):
        rows = part_rows[part]
        if k == 0:
            take(wb.at[pl.ds(0, NY - 1), 0, rows], b_recv.at[part])
            quad(0, 1, 1, part)
            quad(0, 2, -1, part)
            for row in (1, 2, 3):
                w = wb.at[rel[row], 0, rows]
                remote(w, w, b_send.at[3], bs_recv.at[k, part], at(flip=True)).start()
        elif 0 < k < TICKS:
            take(wb.at[all_rows, 2 * k - 1, rows], bz_recv.at[2 * k - 1, part])
            if k < 8:
                quad(2 * k - 1, 2 * k + 1, 1, part)
                take(wb.at[all_rows, 2 * k, rows], bz_recv.at[2 * k, part])
            if k < 7:
                quad(2 * k, 2 * k + 2, -1, part)
            first, count = slots(k)
            w = wb.at[all_rows, pl.ds(first, count), rows]
            remote(w, w, b_send.at[2], bs_recv.at[k, part], at(flip=True)).start()

    def both(k):
        if k == LAG_PART:
            for copy in own_copies:
                copy.wait_recv()
        ring_tick(k, 0)
        ring_tick(k - LAG_PART, 1)
        if k == 0:
            quad_start(0)
        if k == LAG_PART:
            quad_start(1)
        quad_tick(k - 1, 0)
        quad_tick(k - LAG_PART - 1, 1)
        row_tick(k, 0)
        row_tick(k - LAG_PART, 1)

    @pl.when(c == 1)
    def _():
        share_own(len(near))
        both(0)

    loads[0].wait()
    loads[1].wait()

    heads = q_v.shape[1] // HD
    for h in range(heads):
        cols = pl.ds(h * HD, HD)
        v_t = v_v[:, cols].T
        state = jnp.dot(v_t, k_v[:, cols], preferred_element_type=jnp.float32)
        t_own[cols, :] = state
        t_send[cols, :] = state.astype(jnp.bfloat16)

    t_copy = remote(t_send, t_sib, sib_sem.at[0], sib_sem.at[1], at(flip=True))
    pair, second = z // 2, lax.rem(z, 2)
    rows_half = t_own.shape[0] // 2
    mine = pl.ds(pl.multiple_of(second * rows_half, rows_half), rows_half)
    theirs = pl.ds(pl.multiple_of((1 - second) * rows_half, rows_half), rows_half)
    neighbour = at(dz=1 - 2 * second)
    pair_copy = remote(pair_send, pair_in, pair_sem.at[0], pair_sem.at[1], neighbour)
    back_copy = remote(back_send, s_pre.at[mine], pair_sem.at[2], pair_sem.at[3], neighbour)
    s_copy = remote(s_send, s_all, sib_sem.at[2], sib_sem.at[3], at(flip=True))

    before = lax.broadcasted_iota(jnp.int32, (256, 256), 0) <= lax.broadcasted_iota(jnp.int32, (256, 256), 1)

    def inside(h):
        cols = pl.ds(h * HD, HD)
        q_t[cols, :] = q_v[:, cols].T
        scores = jnp.dot(k_v[:, cols], q_t[cols, :], preferred_element_type=jnp.float32)
        scores = jnp.where(before, scores, 0.0).astype(jnp.bfloat16)
        v_t = v_v[:, cols].T
        within[cols, :] = jnp.dot(v_t, scores, preferred_element_type=jnp.float32)
        gain_t[cols, :] = jnp.broadcast_to(gain_v[h : h + 1, :], (HD, HD)).T

    half = heads // 2

    @pl.when(c == 1)
    def _():
        t_copy.start()
        both(1)

    @pl.when(c == 0)
    def _():
        share_own(len(near) + len(far))
        t_copy.wait_recv()
        chip[...] = t_own[...] + t_sib[...].astype(jnp.float32)
        pair_send[...] = chip[theirs, :].astype(jnp.bfloat16)
        pair_copy.start()
        pair_copy.wait_recv()
        both_chips = chip[mine, :] + pair_in[...].astype(jnp.float32)
        c_send[...] = both_chips.astype(jnp.bfloat16).reshape(c_send.shape)
        for d in pair_far:
            remote(
                c_send.at[lax.rem(pair + d // 2, PAIRS)], z_in.at[pair], once_send.at[0], once_recv.at[0], at(dz=d)
            ).start()
        z_in[pair] = c_send[pair]

    loads[2].wait()
    loads[3].wait()
    for h in range(half):
        inside(h)

    @pl.when(c == 1)
    def _():
        both(2)

    for h in range(half, heads):
        inside(h)

    @pl.when(c == 1)
    def _():
        for k in range(3, LAST_EARLY + 1):
            both(k)
        s_copy.wait_recv()

    @pl.when(c == 0)
    def _():
        take(z_in.at[pl.ds(0, PAIRS - 1)], once_recv.at[0])
        total = jnp.zeros(z_in.shape[1:], jnp.float32)
        for j in range(PAIRS):
            pre[j] = total
            total = total + z_in[j].astype(jnp.float32)
        y_in[y] = total.astype(jnp.bfloat16)
        for d in (2, 1, 3):
            remote(y_in.at[y], y_in.at[y], once_send.at[1], once_recv.at[1], at(dy=d)).start()
        take(y_in.at[pl.ds(0, NY - 1)], once_recv.at[1])
        base = jnp.zeros(z_in.shape[1:], jnp.float32)
        for j in range(NY):
            base = base + jnp.where(j < y, y_in[j].astype(jnp.float32), 0.0)
        for j in range(PAIRS):
            p_out[j] = (base + pre[j]).astype(jnp.bfloat16)
        for d in pair_far:
            remote(
                p_out.at[lax.rem(pair + d // 2, PAIRS)], p_half.at[pair], once_send.at[2], once_recv.at[2], at(dz=d)
            ).start()
        p_half[pair] = p_out[pair]
        take(p_half.at[pl.ds(0, PAIRS - 1)], once_recv.at[2])
        before_pair = p_half[...].reshape(pair_in.shape).astype(jnp.float32)
        back_send[...] = (before_pair + jnp.where(second == 0, chip[mine, :], 0.0)).astype(jnp.bfloat16)
        back_copy.start()
        s_pre[mine, :] = (
            before_pair + jnp.where(second == 1, pair_in[...].astype(jnp.float32), 0.0)
        ).astype(jnp.bfloat16)
        back_copy.wait_recv()
        prefix = s_pre[...]
        s_send[...] = (prefix.astype(jnp.float32) + t_own[...]).astype(jnp.bfloat16)
        s_copy.start()
        s_all[...] = prefix
        for copy in own_copies:
            copy.wait_recv()

    for h in range(heads):
        cols = pl.ds(h * HD, HD)
        combined = within[cols, :] + jnp.dot(s_all[cols, :], q_t[cols, :], preferred_element_type=jnp.float32)
        mean = jnp.mean(combined * combined, axis=0, keepdims=True)
        att[cols, :] = (combined * lax.rsqrt(mean + EPS) * gain_t[cols, 0:1]).astype(jnp.bfloat16)

    right, left, across = lax.rem(x + 1, NX), lax.rem(x + NX - 1, NX), lax.rem(x + 2, NX)

    def partial(dest, g):
        first, count = CHUNKS[g]
        a = wa[dest, first : first + count].reshape(64 * count, KA)
        b = wb[dest, first : first + count].reshape(64 * count, wb.shape[-1])
        return jnp.dot(a, att[:KA, :], preferred_element_type=jnp.float32) + jnp.dot(
            b, att[KA:, :], preferred_element_type=jnp.float32
        )

    def x_rows(g):
        first, count = CHUNKS[g]
        return pl.ds(32 * first, 32 * count), 32 * count

    def x2_start(g, way, part, dx):
        rows, _ = x_rows(g)
        remote(
            x2_send.at[way, part, rows], x2_recv.at[way, part, rows], x_send.at[1], x2_sem.at[g, way, part], at(dx=dx)
        ).start()

    def last_tick(g):
        return (CHUNKS[g][0] + CHUNKS[g][1]) // 2

    def arrived(g):
        for t in range(last_tick(g - 1) + 1 if g else 0, last_tick(g) + 1):
            first, count = slots(t)
            for part, rows in enumerate(part_rows):
                take(wb.at[pl.ds(0, NY if t else NY - 1), pl.ds(first, count), rows], bs_recv.at[t, part])
                for row in range(0 if t else 1, 4):
                    take(w_at(row, t, part), ws_recv.at[t, row, part])

    def project(g):
        rows, half_rows = x_rows(g)
        opposite = partial(across, g).astype(jnp.bfloat16)
        for way, dx in ((0, 1), (1, -1)):
            x1_send[way, rows] = opposite[way * half_rows : (way + 1) * half_rows]
            remote(
                x1_send.at[way, rows], x1_recv.at[way, rows], x_send.at[0], x1_sem.at[g, way], at(dx=dx)
            ).start()
        near = partial(right, g)
        x2_send[0, 1, rows] = near[half_rows:].astype(jnp.bfloat16)
        x2_start(g, 0, 1, 1)
        keep[0, rows] = near[:half_rows]
        near = partial(left, g)
        x2_send[1, 0, rows] = near[:half_rows].astype(jnp.bfloat16)
        x2_start(g, 1, 0, -1)
        keep[1, rows] = near[half_rows:]
        own = partial(x, g)
        keep[2, rows] = own[:half_rows]
        keep[3, rows] = own[half_rows:]

    def join(g):
        rows, _ = x_rows(g)
        for way, dx in ((0, 1), (1, -1)):
            take(x1_recv.at[way, rows], x1_sem.at[g, way])
            x2_send[way, way, rows] = (keep[way, rows] + x1_recv[way, rows].astype(jnp.float32)).astype(jnp.bfloat16)
            x2_start(g, way, way, dx)

    def finish(g):
        rows, half_rows = x_rows(g)
        for way, part in ((0, 1), (1, 0), (0, 0), (1, 1)):
            take(x2_recv.at[way, part, rows], x2_sem.at[g, way, part])
        for part in range(2):
            total = keep[2 + part, rows] + (
                x2_recv[0, part, rows].astype(jnp.float32) + x2_recv[1, part, rows].astype(jnp.float32)
            )
            total = total.astype(jnp.bfloat16)
            for i in range(half_rows // 32):
                unit = 2 * CHUNKS[g][0] + part * (half_rows // 32) + i
                slot, core = unit // 2, unit % 2
                step = (slot + 1) // 2
                where = lax.rem(z + NZ + (-step if slot % 2 == 1 else step) * LONG_WAY, NZ)
                out_t[pl.ds(pl.multiple_of(where * 64 + core * 32, 32), 32), :] = total[32 * i : 32 * i + 32]

    done = LAST_EARLY
    count = len(CHUNKS)
    for g in range(count):
        need = max(done, last_tick(g) + LAG_PART + LAG_FAR)

        @pl.when(c == 1)
        def _():
            for k in range(done + 1, need + 1):
                both(k)

        @pl.when(c == 0)
        def _():
            arrived(g)

        done = need
        project(g)
        if g >= 1:
            join(g - 1)
        if g >= 2:
            finish(g - 2)
    join(count - 1)
    finish(count - 2)
    finish(count - 1)
    out_ref[...] = out_t[...].T

    for copy in own_copies:
        copy.wait_send()
    take(x1_recv, x_send.at[0])
    take(x2_recv, x_send.at[1])

    @pl.when(c == 0)
    def _():
        s_copy.wait_send()
        pair_copy.wait_send()
        back_copy.wait_send()
        take(z_in.at[pl.ds(0, PAIRS - 1)], once_send.at[0])
        take(y_in.at[pl.ds(0, NY - 1)], once_send.at[1])
        take(p_half.at[pl.ds(0, PAIRS - 1)], once_send.at[2])

    @pl.when(c == 1)
    def _():
        t_copy.wait_send()
        take(wa.at[0, pl.ds(0, 15)], w_send.at[0])
        take(wa.at[pl.ds(0, 2)], w_send.at[1])
        take(wa.at[0], w_send.at[2])
        take(wa.at[pl.ds(0, 3)], w_send.at[3])
        take(wa.at[0, pl.ds(0, 15)], w_send.at[4])
        take(wb.at[pl.ds(0, NY - 1), 0], b_send.at[0])
        take(wb.at[:, pl.ds(0, 15)], b_send.at[1])
        take(wb.at[pl.ds(0, NY - 1), 0], b_send.at[3])
        take(wb.at[:, pl.ds(0, 15)], b_send.at[2])


def body(queries, key_vectors, value_vectors, norm_gain, out_weight):
    tokens, features = queries.shape
    heads = features // HD
    bf16, f32 = jnp.bfloat16, jnp.float32
    sem = pltpu.SemaphoreType.DMA
    anywhere = pl.BlockSpec(memory_space=pl.ANY)
    return pl.pallas_call(
        kernel,
        out_shape=jax.ShapeDtypeStruct((tokens, features), bf16),
        in_specs=[anywhere] * 5,
        out_specs=pl.BlockSpec(memory_space=pltpu.VMEM),
        scratch_shapes=[
            pltpu.VMEM((tokens, features), bf16),
            pltpu.VMEM((tokens, features), bf16),
            pltpu.VMEM((tokens, features), bf16),
            pltpu.VMEM((heads, HD), f32),
            pltpu.VMEM((features, tokens), bf16),
            pltpu.VMEM((features, tokens), f32),
            pltpu.VMEM((features, HD), f32),
            pltpu.VMEM((features, HD), f32),
            pltpu.VMEM((features, HD), bf16),
            pltpu.VMEM((features, HD), bf16),
            pltpu.VMEM((features, HD), f32),
            pltpu.VMEM((features // 2, HD), bf16),
            pltpu.VMEM((features // 2, HD), bf16),
            pltpu.VMEM((features // 2, HD), bf16),
            pltpu.VMEM((features, HD), bf16),
            pltpu.VMEM((PAIRS, features // NZ, HD), bf16),
            pltpu.VMEM((PAIRS, features // NZ, HD), bf16),
            pltpu.VMEM((PAIRS, features // NZ, HD), f32),
            pltpu.VMEM((NY, features // NZ, HD), bf16),
            pltpu.VMEM((PAIRS, features // NZ, HD), bf16),
            pltpu.VMEM((PAIRS, features // NZ, HD), bf16),
            pltpu.VMEM((features, HD), bf16),
            pltpu.VMEM((features, HD), bf16),
            pltpu.VMEM((features, tokens), bf16),
            pltpu.VMEM((NY, NZ, 64, KA), bf16),
            pltpu.VMEM((NY, NZ, 64, features - KA), bf16),
            pltpu.VMEM((2, features // 2, tokens), bf16),
            pltpu.VMEM((2, features // 2, tokens), bf16),
            pltpu.VMEM((2, 2, features // 2, tokens), bf16),
            pltpu.VMEM((2, 2, features // 2, tokens), bf16),
            pltpu.VMEM((4, features // 2, tokens), f32),
            pltpu.VMEM((features, tokens), bf16),
            sem((6,)),
            sem((4,)),
            sem((4,)),
            sem((4,)),
            sem((3,)),
            sem((3,)),
            sem((16, 2)),
            sem((TICKS, 2)),
            sem((TICKS, 2)),
            sem((16, 2)),
            sem((TICKS, 4, 2)),
            sem((5,)),
            sem((2,)),
            sem((16, 2)),
            sem((TICKS, 2)),
            sem((4,)),
            sem((len(CHUNKS), 2)),
            sem((len(CHUNKS), 2, 2)),
            sem((2,)),
        ],
        compiler_params=pltpu.CompilerParams(
            collective_id=0, has_side_effects=True, vmem_limit_bytes=62 << 20
        ),
        cost_estimate=pl.CostEstimate(flops=2_550_000_000, bytes_accessed=12_000_000, transcendentals=4096),
        name="attend_and_project",
    )(queries, key_vectors, value_vectors, norm_gain.reshape(heads, HD), out_weight.T)


def solution(mesh):
    in_specs = (P("seq", "head"), P("seq", "head"), P("seq", "head"), P("head"), P("head", "seq"))
    return jax.shard_map(body, mesh=mesh, in_specs=in_specs, out_specs=P("seq", "head"), check_vma=False)
```

```python
import jax
import jax.numpy as jnp
from jax import lax
from jax.experimental import pallas as pl
from jax.experimental.pallas import tpu as pltpu
from jax.sharding import PartitionSpec as P

HD = 128
NY, NZ, NX = 4, 16, 4
EPS = 1e-06
MESH = pl.DeviceIdType.MESH
PAIRS = NZ // 2
TICKS = 9
LAG_NEAR, LAG_FAR = 2, 4
KA = 896
LAG_PART = 2
LONG_WAY = 1
CHUNKS = ((0, 4), (4, 4), (8, 4), (12, 3), (15, 1))
LAST_EARLY = 10


def slots(tick):
    if tick == 0:
        return 0, 1
    if tick == 8:
        return 15, 1
    return 2 * tick - 1, 2


def kernel(
    q_hbm, k_hbm, v_hbm, gain_hbm, w_hbm, out_ref,
    q_v, k_v, v_v, gain_v, q_t, within, gain_t, t_own, t_send, t_sib, chip, pair_send, pair_in, back_send, s_pre, c_send, z_in, pre, y_in,
    p_out, p_half, s_send, s_all, att, wa, wb, x1_send, x1_recv, x2_send, x2_recv, keep, out_t,
    load_sem, sib_sem, own_sem, pair_sem, once_send, once_recv, wz_recv, wl_recv, wr_recv, w2_recv, ws_recv, w_send,
    b_recv, bz_recv, bs_recv, b_send, x1_sem, x2_sem, x_send,
):
    s = lax.axis_index("seq")
    x = lax.axis_index("head")
    c = lax.rem(s, 2)
    z = lax.rem(s // 2, NZ)
    y = s // (2 * NZ)

    def at(dy=0, dz=0, dx=0, flip=False):
        yy, zz = lax.rem(y + dy + NY, NY), lax.rem(z + dz + NZ, NZ)
        return ((yy * NZ + zz) * 2 + (1 - c if flip else c), lax.rem(x + dx + NX, NX))

    def remote(src, dst, send, recv, device):
        return pltpu.make_async_remote_copy(
            src_ref=src, dst_ref=dst, send_sem=send, recv_sem=recv, device_id=device, device_id_type=MESH
        )

    def take(ref, sem):
        pltpu.make_async_copy(ref, ref, sem).wait()

    pair_far = [8, 6, 10, 4, 12, 2, 14]
    barrier = pltpu.get_barrier_semaphore()
    near = [at(dz=1), at(dz=-1), at(dy=1), at(dy=2), at(dy=3), at(dx=1), at(dx=-1), at(flip=True)]
    far = [at(dz=d) for d in pair_far]

    def greet(partners):
        for partner in partners:
            pl.semaphore_signal(barrier, inc=1, device_id=partner, device_id_type=MESH)

    @pl.when(c == 0)
    def _():
        greet(far)

    greet(near)

    own_rows = pl.ds(pl.multiple_of(c * 32, 32), 32)
    loads = [
        pltpu.make_async_copy(v_hbm, v_v, load_sem.at[0]),
        pltpu.make_async_copy(k_hbm, k_v, load_sem.at[1]),
        pltpu.make_async_copy(q_hbm, q_v, load_sem.at[2]),
        pltpu.make_async_copy(gain_hbm, gain_v, load_sem.at[3]),
        pltpu.make_async_copy(w_hbm.at[:, pl.ds(0, KA)], wa.at[y, 0, own_rows], load_sem.at[4]),
        pltpu.make_async_copy(w_hbm.at[:, pl.ds(KA, wb.shape[-1])], wb.at[y, 0, own_rows], load_sem.at[5]),
    ]
    for load in loads:
        load.start()
    own_copies = [
        remote(w.at[y, 0, own_rows], w.at[y, 0, own_rows], own_sem.at[i], own_sem.at[2 + i], at(flip=True))
        for i, w in enumerate((wa, wb))
    ]

    def share_own(partners):
        loads[4].wait()
        loads[5].wait()
        pl.semaphore_wait(barrier, partners)
        for copy in own_copies:
            copy.start()

    rel = [y, lax.rem(y + NY - 1, NY), lax.rem(y + 1, NY), lax.rem(y + 2, NY)]

    part_rows = (pl.ds(32, 32), pl.ds(0, 32))

    def w_at(row, tick, part):
        first, count = slots(tick)
        return wa.at[rel[row], pl.ds(first, count), part_rows[part]]

    def to_sibling(row, tick, part):
        w = w_at(row, tick, part)
        remote(w, w, w_send.at[3 if row else 4], ws_recv.at[tick, row, part], at(flip=True)).start()

    def along_z(slot_from, slot_to, dz, part):
        rows = part_rows[part]
        remote(
            wa.at[y, slot_from, rows], wa.at[y, slot_to, rows], w_send.at[0], wz_recv.at[slot_to, part], at(dz=dz * LONG_WAY)
        ).start()

    def ring_tick(k, part):
        if k == 0:
            along_z(0, 1, 1, part)
            along_z(0, 2, -1, part)
        elif 0 < k < TICKS:
            take(wa.at[y, 2 * k - 1, part_rows[part]], wz_recv.at[2 * k - 1, part])
            if k < 8:
                along_z(2 * k - 1, 2 * k + 1, 1, part)
                take(wa.at[y, 2 * k, part_rows[part]], wz_recv.at[2 * k, part])
            if k < 7:
                along_z(2 * k, 2 * k + 2, -1, part)

    def row_tick(k, part):
        if 0 <= k < TICKS:
            w = w_at(0, k, part)
            remote(w, w, w_send.at[1], wl_recv.at[k, part], at(dy=1)).start()
            remote(w, w, w_send.at[1], wr_recv.at[k, part], at(dy=-1)).start()
            if k:
                to_sibling(0, k, part)
        j = k - LAG_NEAR
        if 0 <= j < TICKS:
            first, count = slots(j)
            take(w_at(1, j, part), wl_recv.at[j, part])
            for slot in range(first, first + count):
                if slot % 2 == 0:
                    w = wa.at[rel[1], slot, part_rows[part]]
                    remote(w, w, w_send.at[2], w2_recv.at[slot, part], at(dy=1)).start()
            to_sibling(1, j, part)
            take(w_at(2, j, part), wr_recv.at[j, part])
            for slot in range(first, first + count):
                if slot % 2 == 1:
                    w = wa.at[rel[2], slot, part_rows[part]]
                    remote(w, w, w_send.at[2], w2_recv.at[slot, part], at(dy=-1)).start()
            to_sibling(2, j, part)
        j = k - LAG_FAR
        if 0 <= j < TICKS:
            first, count = slots(j)
            for slot in range(first, first + count):
                take(wa.at[rel[3], slot, part_rows[part]], w2_recv.at[slot, part])
            to_sibling(3, j, part)

    all_rows = pl.ds(0, NY)

    def quad_start(part):
        own = wb.at[y, 0, part_rows[part]]
        for d in (1, 3, 2):
            remote(own, own, b_send.at[0], b_recv.at[part], at(dy=d)).start()

    def quad(slot_from, slot_to, dz, part):
        rows = part_rows[part]
        remote(
            wb.at[all_rows, slot_from, rows], wb.at[all_rows, slot_to, rows],
            b_send.at[1], bz_recv.at[slot_to, part], at(dz=dz * LONG_WAY),
        ).start()

    def quad_tick(k, part):
        rows = part_rows[part]
        if k == 0:
            take(wb.at[pl.ds(0, NY - 1), 0, rows], b_recv.at[part])
            quad(0, 1, 1, part)
            quad(0, 2, -1, part)
            for row in (1, 2, 3):
                w = wb.at[rel[row], 0, rows]
                remote(w, w, b_send.at[3], bs_recv.at[k, part], at(flip=True)).start()
        elif 0 < k < TICKS:
            take(wb.at[all_rows, 2 * k - 1, rows], bz_recv.at[2 * k - 1, part])
            if k < 8:
                quad(2 * k - 1, 2 * k + 1, 1, part)
                take(wb.at[all_rows, 2 * k, rows], bz_recv.at[2 * k, part])
            if k < 7:
                quad(2 * k, 2 * k + 2, -1, part)
            first, count = slots(k)
            w = wb.at[all_rows, pl.ds(first, count), rows]
            remote(w, w, b_send.at[2], bs_recv.at[k, part], at(flip=True)).start()

    def both(k):
        if k == LAG_PART:
            for copy in own_copies:
                copy.wait_recv()
        ring_tick(k, 0)
        ring_tick(k - LAG_PART, 1)
        if k == 0:
            quad_start(0)
        if k == LAG_PART:
            quad_start(1)
        quad_tick(k - 1, 0)
        quad_tick(k - LAG_PART - 1, 1)
        row_tick(k, 0)
        row_tick(k - LAG_PART, 1)

    @pl.when(c == 1)
    def _():
        share_own(len(near))
        both(0)

    loads[0].wait()
    loads[1].wait()

    heads = q_v.shape[1] // HD
    for h in range(heads):
        cols = pl.ds(h * HD, HD)
        v_t = v_v[:, cols].T
        state = jnp.dot(v_t, k_v[:, cols], preferred_element_type=jnp.float32)
        t_own[cols, :] = state
        t_send[cols, :] = state.astype(jnp.bfloat16)

    t_copy = remote(t_send, t_sib, sib_sem.at[0], sib_sem.at[1], at(flip=True))
    pair, second = z // 2, lax.rem(z, 2)
    rows_half = t_own.shape[0] // 2
    mine = pl.ds(pl.multiple_of(second * rows_half, rows_half), rows_half)
    theirs = pl.ds(pl.multiple_of((1 - second) * rows_half, rows_half), rows_half)
    neighbour = at(dz=1 - 2 * second)
    pair_copy = remote(pair_send, pair_in, pair_sem.at[0], pair_sem.at[1], neighbour)
    back_copy = remote(back_send, s_pre.at[mine], pair_sem.at[2], pair_sem.at[3], neighbour)
    s_copy = remote(s_send, s_all, sib_sem.at[2], sib_sem.at[3], at(flip=True))

    before = lax.broadcasted_iota(jnp.int32, (256, 256), 0) <= lax.broadcasted_iota(jnp.int32, (256, 256), 1)

    def inside(h):
        cols = pl.ds(h * HD, HD)
        q_t[cols, :] = q_v[:, cols].T
        scores = jnp.dot(k_v[:, cols], q_t[cols, :], preferred_element_type=jnp.float32)
        scores = jnp.where(before, scores, 0.0).astype(jnp.bfloat16)
        v_t = v_v[:, cols].T
        within[cols, :] = jnp.dot(v_t, scores, preferred_element_type=jnp.float32)
        gain_t[cols, :] = jnp.broadcast_to(gain_v[h : h + 1, :], (HD, HD)).T

    half = heads // 2

    @pl.when(c == 1)
    def _():
        t_copy.start()
        both(1)

    @pl.when(c == 0)
    def _():
        share_own(len(near) + len(far))
        t_copy.wait_recv()
        chip[...] = t_own[...] + t_sib[...].astype(jnp.float32)
        pair_send[...] = chip[theirs, :].astype(jnp.bfloat16)
        pair_copy.start()
        pair_copy.wait_recv()
        both_chips = chip[mine, :] + pair_in[...].astype(jnp.float32)
        c_send[...] = both_chips.astype(jnp.bfloat16).reshape(c_send.shape)
        for d in pair_far:
            remote(
                c_send.at[lax.rem(pair + d // 2, PAIRS)], z_in.at[pair], once_send.at[0], once_recv.at[0], at(dz=d)
            ).start()
        z_in[pair] = c_send[pair]

    loads[2].wait()
    loads[3].wait()
    for h in range(half):
        inside(h)

    @pl.when(c == 1)
    def _():
        both(2)

    for h in range(half, heads):
        inside(h)

    @pl.when(c == 1)
    def _():
        for k in range(3, LAST_EARLY + 1):
            both(k)
        s_copy.wait_recv()

    @pl.when(c == 0)
    def _():
        take(z_in.at[pl.ds(0, PAIRS - 1)], once_recv.at[0])
        total = jnp.zeros(z_in.shape[1:], jnp.float32)
        for j in range(PAIRS):
            pre[j] = total
            total = total + z_in[j].astype(jnp.float32)
        y_in[y] = total.astype(jnp.bfloat16)
        for d in (2, 1, 3):
            remote(y_in.at[y], y_in.at[y], once_send.at[1], once_recv.at[1], at(dy=d)).start()
        take(y_in.at[pl.ds(0, NY - 1)], once_recv.at[1])
        base = jnp.zeros(z_in.shape[1:], jnp.float32)
        for j in range(NY):
            base = base + jnp.where(j < y, y_in[j].astype(jnp.float32), 0.0)
        for j in range(PAIRS):
            p_out[j] = (base + pre[j]).astype(jnp.bfloat16)
        for d in pair_far:
            remote(
                p_out.at[lax.rem(pair + d // 2, PAIRS)], p_half.at[pair], once_send.at[2], once_recv.at[2], at(dz=d)
            ).start()
        p_half[pair] = p_out[pair]
        take(p_half.at[pl.ds(0, PAIRS - 1)], once_recv.at[2])
        before_pair = p_half[...].reshape(pair_in.shape).astype(jnp.float32)
        back_send[...] = (before_pair + jnp.where(second == 0, chip[mine, :], 0.0)).astype(jnp.bfloat16)
        back_copy.start()
        s_pre[mine, :] = (
            before_pair + jnp.where(second == 1, pair_in[...].astype(jnp.float32), 0.0)
        ).astype(jnp.bfloat16)
        back_copy.wait_recv()
        prefix = s_pre[...]
        s_send[...] = (prefix.astype(jnp.float32) + t_own[...]).astype(jnp.bfloat16)
        s_copy.start()
        s_all[...] = prefix
        for copy in own_copies:
            copy.wait_recv()

    for h in range(heads):
        cols = pl.ds(h * HD, HD)
        combined = within[cols, :] + jnp.dot(s_all[cols, :], q_t[cols, :], preferred_element_type=jnp.float32)
        mean = jnp.mean(combined * combined, axis=0, keepdims=True)
        att[cols, :] = (combined * lax.rsqrt(mean + EPS) * gain_t[cols, 0:1]).astype(jnp.bfloat16)

    right, left, across = lax.rem(x + 1, NX), lax.rem(x + NX - 1, NX), lax.rem(x + 2, NX)

    def partial(dest, g):
        first, count = CHUNKS[g]
        a = wa[dest, first : first + count].reshape(64 * count, KA)
        b = wb[dest, first : first + count].reshape(64 * count, wb.shape[-1])
        return jnp.dot(a, att[:KA, :], preferred_element_type=jnp.float32) + jnp.dot(
            b, att[KA:, :], preferred_element_type=jnp.float32
        )

    def x_rows(g):
        first, count = CHUNKS[g]
        return pl.ds(32 * first, 32 * count), 32 * count

    def x2_start(g, way, part, dx):
        rows, _ = x_rows(g)
        remote(
            x2_send.at[way, part, rows], x2_recv.at[way, part, rows], x_send.at[1], x2_sem.at[g, way, part], at(dx=dx)
        ).start()

    def last_tick(g):
        return (CHUNKS[g][0] + CHUNKS[g][1]) // 2

    def arrived(g):
        for t in range(last_tick(g - 1) + 1 if g else 0, last_tick(g) + 1):
            first, count = slots(t)
            for part, rows in enumerate(part_rows):
                take(wb.at[pl.ds(0, NY if t else NY - 1), pl.ds(first, count), rows], bs_recv.at[t, part])
                for row in range(0 if t else 1, 4):
                    take(w_at(row, t, part), ws_recv.at[t, row, part])

    def project(g):
        rows, half_rows = x_rows(g)
        opposite = partial(across, g).astype(jnp.bfloat16)
        for way, dx in ((0, 1), (1, -1)):
            x1_send[way, rows] = opposite[way * half_rows : (way + 1) * half_rows]
            remote(
                x1_send.at[way, rows], x1_recv.at[way, rows], x_send.at[0], x1_sem.at[g, way], at(dx=dx)
            ).start()
        near = partial(right, g)
        x2_send[0, 1, rows] = near[half_rows:].astype(jnp.bfloat16)
        x2_start(g, 0, 1, 1)
        keep[0, rows] = near[:half_rows]
        near = partial(left, g)
        x2_send[1, 0, rows] = near[:half_rows].astype(jnp.bfloat16)
        x2_start(g, 1, 0, -1)
        keep[1, rows] = near[half_rows:]
        own = partial(x, g)
        keep[2, rows] = own[:half_rows]
        keep[3, rows] = own[half_rows:]

    def join(g):
        rows, _ = x_rows(g)
        for way, dx in ((0, 1), (1, -1)):
            take(x1_recv.at[way, rows], x1_sem.at[g, way])
            x2_send[way, way, rows] = (keep[way, rows] + x1_recv[way, rows].astype(jnp.float32)).astype(jnp.bfloat16)
            x2_start(g, way, way, dx)

    def finish(g):
        rows, half_rows = x_rows(g)
        for way, part in ((0, 1), (1, 0), (0, 0), (1, 1)):
            take(x2_recv.at[way, part, rows], x2_sem.at[g, way, part])
        for part in range(2):
            total = keep[2 + part, rows] + (
                x2_recv[0, part, rows].astype(jnp.float32) + x2_recv[1, part, rows].astype(jnp.float32)
            )
            total = total.astype(jnp.bfloat16)
            for i in range(half_rows // 32):
                unit = 2 * CHUNKS[g][0] + part * (half_rows // 32) + i
                slot, core = unit // 2, unit % 2
                step = (slot + 1) // 2
                where = lax.rem(z + NZ + (-step if slot % 2 == 1 else step) * LONG_WAY, NZ)
                out_t[pl.ds(pl.multiple_of(where * 64 + core * 32, 32), 32), :] = total[32 * i : 32 * i + 32]

    done = LAST_EARLY
    count = len(CHUNKS)
    for g in range(count):
        need = max(done, last_tick(g) + LAG_PART + LAG_FAR)

        @pl.when(c == 1)
        def _():
            for k in range(done + 1, need + 1):
                both(k)

        @pl.when(c == 0)
        def _():
            arrived(g)

        done = need
        project(g)
        if g >= 1:
            join(g - 1)
        if g >= 2:
            finish(g - 2)
    join(count - 1)
    finish(count - 2)
    finish(count - 1)
    out_ref[...] = out_t[...].T

    for copy in own_copies:
        copy.wait_send()
    take(x1_recv, x_send.at[0])
    take(x2_recv, x_send.at[1])

    @pl.when(c == 0)
    def _():
        s_copy.wait_send()
        pair_copy.wait_send()
        back_copy.wait_send()
        take(z_in.at[pl.ds(0, PAIRS - 1)], once_send.at[0])
        take(y_in.at[pl.ds(0, NY - 1)], once_send.at[1])
        take(p_half.at[pl.ds(0, PAIRS - 1)], once_send.at[2])

    @pl.when(c == 1)
    def _():
        t_copy.wait_send()
        take(wa.at[0, pl.ds(0, 15)], w_send.at[0])
        take(wa.at[pl.ds(0, 2)], w_send.at[1])
        take(wa.at[0], w_send.at[2])
        take(wa.at[pl.ds(0, 3)], w_send.at[3])
        take(wa.at[0, pl.ds(0, 15)], w_send.at[4])
        take(wb.at[pl.ds(0, NY - 1), 0], b_send.at[0])
        take(wb.at[:, pl.ds(0, 15)], b_send.at[1])
        take(wb.at[pl.ds(0, NY - 1), 0], b_send.at[3])
        take(wb.at[:, pl.ds(0, 15)], b_send.at[2])


def body(queries, key_vectors, value_vectors, norm_gain, out_weight):
    tokens, features = queries.shape
    heads = features // HD
    bf16, f32 = jnp.bfloat16, jnp.float32
    sem = pltpu.SemaphoreType.DMA
    anywhere = pl.BlockSpec(memory_space=pl.ANY)
    return pl.pallas_call(
        kernel,
        out_shape=jax.ShapeDtypeStruct((tokens, features), bf16),
        in_specs=[anywhere] * 5,
        out_specs=pl.BlockSpec(memory_space=pltpu.VMEM),
        scratch_shapes=[
            pltpu.VMEM((tokens, features), bf16),
            pltpu.VMEM((tokens, features), bf16),
            pltpu.VMEM((tokens, features), bf16),
            pltpu.VMEM((heads, HD), f32),
            pltpu.VMEM((features, tokens), bf16),
            pltpu.VMEM((features, tokens), f32),
            pltpu.VMEM((features, HD), f32),
            pltpu.VMEM((features, HD), f32),
            pltpu.VMEM((features, HD), bf16),
            pltpu.VMEM((features, HD), bf16),
            pltpu.VMEM((features, HD), f32),
            pltpu.VMEM((features // 2, HD), bf16),
            pltpu.VMEM((features // 2, HD), bf16),
            pltpu.VMEM((features // 2, HD), bf16),
            pltpu.VMEM((features, HD), bf16),
            pltpu.VMEM((PAIRS, features // NZ, HD), bf16),
            pltpu.VMEM((PAIRS, features // NZ, HD), bf16),
            pltpu.VMEM((PAIRS, features // NZ, HD), f32),
            pltpu.VMEM((NY, features // NZ, HD), bf16),
            pltpu.VMEM((PAIRS, features // NZ, HD), bf16),
            pltpu.VMEM((PAIRS, features // NZ, HD), bf16),
            pltpu.VMEM((features, HD), bf16),
            pltpu.VMEM((features, HD), bf16),
            pltpu.VMEM((features, tokens), bf16),
            pltpu.VMEM((NY, NZ, 64, KA), bf16),
            pltpu.VMEM((NY, NZ, 64, features - KA), bf16),
            pltpu.VMEM((2, features // 2, tokens), bf16),
            pltpu.VMEM((2, features // 2, tokens), bf16),
            pltpu.VMEM((2, 2, features // 2, tokens), bf16),
            pltpu.VMEM((2, 2, features // 2, tokens), bf16),
            pltpu.VMEM((4, features // 2, tokens), f32),
            pltpu.VMEM((features, tokens), bf16),
            sem((6,)),
            sem((4,)),
            sem((4,)),
            sem((4,)),
            sem((3,)),
            sem((3,)),
            sem((16, 2)),
            sem((TICKS, 2)),
            sem((TICKS, 2)),
            sem((16, 2)),
            sem((TICKS, 4, 2)),
            sem((5,)),
            sem((2,)),
            sem((16, 2)),
            sem((TICKS, 2)),
            sem((4,)),
            sem((len(CHUNKS), 2)),
            sem((len(CHUNKS), 2, 2)),
            sem((2,)),
        ],
        compiler_params=pltpu.CompilerParams(
            collective_id=0, has_side_effects=True, vmem_limit_bytes=62 << 20
        ),
        cost_estimate=pl.CostEstimate(flops=2_550_000_000, bytes_accessed=12_000_000, transcendentals=4096),
        name="attend_and_project",
    )(queries, key_vectors, value_vectors, norm_gain.reshape(heads, HD), out_weight.T)


def solution(mesh):
    in_specs = (P("seq", "head"), P("seq", "head"), P("seq", "head"), P("head"), P("head", "seq"))
    return jax.shard_map(body, mesh=mesh, in_specs=in_specs, out_specs=P("seq", "head"), check_vma=False)
```
